32 devices in a mesh: ga: 4 (over z), pa: 8 (over y, x, core).
Axes of the slice: x: 2, y: 2, z: 4, core: 2. Of those that a mesh axis runs over, the one named last changes fastest.
Arguments:
- pair_matrix: bfloat16 [2, 6144, 4096], P(None, 'pa', 'ga'), may hold values from -0.0390625 to 0.0390625
- valence_idx: int32 [6144], P('pa'), may hold values from 0 to 2047
- conduction_idx: int32 [6144], P('pa'), may hold values from 0 to 4095
- e_val: float32 [2048], replicated, may hold values from -6 to -0.1
- e_cond: float32 [4096], replicated, may hold values from 0.1 to 6
Outputs:
- chi_real: float32 [2, 4096, 4096], P(None, ('ga', 'pa'))
- chi_imag: float32 [2, 4096, 4096], P(None, ('ga', 'pa'))
The draws below stay inside these ranges and needn't reach their ends.
All inputs are finite; a program needn't handle non-finite values.
Results may differ from the reference program's by a relative error of at most 0.0095.
Values may be sent and summed in bfloat16 or wider, within the bound.
A program may use at most 128 MiB of HBM per device.

```python
import jax
import jax.numpy as jnp
from jax import lax

GVECS = 4096
PAIRS_DEV = 768
NVAL = 2048
NCOND = 4096
PAIRS = 6144
N_PA = 8


def set_ends(drawn, key, least, top_value):
    extent = drawn.shape
    place = [jax.random.randint(jax.random.fold_in(key, axis), (), 0, extent[axis]) for axis in range(len(extent))]
    drawn = drawn.at[tuple(place)].set(least)
    longest = extent.index(max(extent))
    place[longest] = (place[longest] + 1) % extent[longest]
    return drawn.at[tuple(place)].set(top_value)


def shard_levels(rng, shape, shards, low, top_value):
    def one(axis_at, parts):
        steps = jax.random.uniform(jax.random.fold_in(jax.random.fold_in(rng, 6), axis_at), (parts,), jnp.float32, low / len(shards), top_value / len(shards))
        return jnp.repeat(jnp.exp(steps), shape[axis_at] // parts).reshape((-1,) + (1,) * (len(shape) - axis_at - 1))

    loudness = one(*shards[0])
    for cut in shards[1:]:
        loudness = loudness * one(*cut)
    return loudness


def bell_draw(stream_key, dims, width, limit, shards=(), held_as=jnp.bfloat16):
    entries = jax.random.normal(stream_key, dims, jnp.float32) * width
    if len(shards) > 0:
        entries = shard_levels(stream_key, dims, shards, -0.22, 0.18) * entries
    return jnp.clip(entries, min=-limit, max=limit).astype(held_as)


def setup_inputs(seed: int = 0) -> dict:
    splits = jax.random.split(jax.random.key(seed), 6)
    return {
        "pair_matrix": bell_draw(splits[0], (2, PAIRS, GVECS), (4 * PAIRS) ** -0.5, 0.0390625, ((1, 8), (2, 4))),
        "valence_idx": set_ends(jax.random.randint(splits[1], (PAIRS,), 0, NVAL), jax.random.fold_in(splits[1], 1), 0, NVAL - 1).astype(jnp.int32),
        "conduction_idx": set_ends(jax.random.randint(splits[2], (PAIRS,), 0, NCOND), jax.random.fold_in(splits[2], 1), 0, NCOND - 1).astype(jnp.int32),
        "e_val": jnp.clip(jax.random.uniform(splits[3], (NVAL,), jnp.float32, -6.0, -0.1), -6.0, -0.1),
        "e_cond": jnp.clip(jax.random.uniform(splits[4], (NCOND,), jnp.float32, 0.1, 6.0), 0.1, 6.0),
    }


omega_squared = 4.0


def reference(pair_matrix, valence_idx, conduction_idx, e_val, e_cond):
    gap = e_cond[conduction_idx] - e_val[valence_idx]
    static_w = -4.0 / gap
    dynamic_w = -4.0 * gap / (gap * gap + omega_squared)

    def add_block(acc, index):
        start = (index * PAIRS_DEV).astype(jnp.int32)
        block = lax.dynamic_slice_in_dim(pair_matrix, start, PAIRS_DEV, 1)
        swt = lax.dynamic_slice_in_dim(static_w, start, PAIRS_DEV, 0)[:, None]
        dwt = lax.dynamic_slice_in_dim(dynamic_w, start, PAIRS_DEV, 0)[:, None]
        re32 = block[0].astype(jnp.float32)
        im32 = block[1].astype(jnp.float32)
        real_rhs = jnp.concatenate([jnp.concatenate([swt * re32, dwt * re32], 1),
                                    jnp.concatenate([swt * im32, dwt * im32], 1)], 0).astype(jnp.bfloat16)
        imag_rhs = jnp.concatenate([jnp.concatenate([swt * im32, dwt * im32], 1),
                                    jnp.concatenate([-(swt * re32), -(dwt * re32)], 1)], 0).astype(jnp.bfloat16)
        left = jnp.concatenate([block[0], block[1]], 0).astype(jnp.float32)
        first = jnp.dot(left.T, real_rhs.astype(jnp.float32), precision=lax.Precision.HIGHEST,
                        preferred_element_type=jnp.float32)
        second = jnp.dot(left.T, imag_rhs.astype(jnp.float32), precision=lax.Precision.HIGHEST,
                         preferred_element_type=jnp.float32)
        term = jnp.concatenate([first, second], 1).astype(jnp.bfloat16)
        term = lax.optimization_barrier(term)
        return acc + term.astype(jnp.float32), None

    start_acc = jnp.zeros((GVECS, 4 * GVECS), jnp.float32)
    total, _ = lax.scan(add_block, start_acc, jnp.arange(N_PA, dtype=jnp.int32))
    total = total.reshape(GVECS, 2, 2, GVECS)
    chi_real = jnp.transpose(total[:, 0], (1, 0, 2))
    chi_imag = jnp.transpose(total[:, 1], (1, 0, 2))
    return (chi_real, chi_imag)
```

```python
import jax
import jax.numpy as jnp
from jax import lax
from jax.sharding import PartitionSpec as P

omega_squared = 4.0


def pair_weights(valence_idx, conduction_idx, e_val, e_cond):
    val_hits = valence_idx[:, None] == jnp.arange(e_val.shape[0], dtype=jnp.int32)[None, :]
    cond_hits = conduction_idx[:, None] == jnp.arange(e_cond.shape[0], dtype=jnp.int32)[None, :]
    picked_val = jnp.sum(jnp.where(val_hits, e_val[None, :], 0.0), 1)
    picked_cond = jnp.sum(jnp.where(cond_hits, e_cond[None, :], 0.0), 1)
    gap = picked_cond - picked_val
    return jnp.stack([-4.0 / gap, -4.0 * gap / (gap * gap + omega_squared)])


def local(pair_matrix, valence_idx, conduction_idx, e_val, e_cond):
    n_ga, n_pa = lax.axis_size("ga"), lax.axis_size("pa")
    g, p = lax.axis_index("ga"), lax.axis_index("pa")
    n_chip = n_pa // 2
    chip, core = p // 2, p % 2
    gblock = pair_matrix.shape[2]
    out_rows = gblock // n_pa
    chip_rows = 2 * out_rows
    half = gblock // 2
    bf16, f32 = jnp.bfloat16, jnp.float32

    walk = list(range(n_chip // 2)) + list(range(n_chip - 1, n_chip // 2 - 1, -1))
    place_of = [walk.index(c) for c in range(n_chip)]
    walk_table = jnp.array(walk, jnp.int32)
    spot = jnp.array(place_of, jnp.int32)[chip]
    way = 1 - 2 * core
    ring_route = []
    for i in range(n_chip):
        ring_route.append((2 * walk[i], 2 * walk[(i + 1) % n_chip]))
        ring_route.append((2 * walk[i] + 1, 2 * walk[(i - 1) % n_chip] + 1))
    sibling_route = [(i, i ^ 1) for i in range(n_pa)]

    def core_columns(x):
        parts = x.reshape(x.shape[:-1] + (n_chip, 2, out_rows))
        picked = jnp.where(core == 0, parts[..., 0, :], parts[..., 1, :])
        return picked.reshape(x.shape[:-1] + (half,))

    sibling = lax.ppermute(pair_matrix, "pa", sibling_route)
    weight = pair_weights(valence_idx, conduction_idx, e_val, e_cond)
    weight = jnp.concatenate([weight, lax.ppermute(weight, "pa", sibling_route)], 1)

    own_cols = jnp.concatenate([core_columns(pair_matrix), core_columns(sibling)], 1)
    pairs = own_cols.shape[1]
    own_cols = own_cols.reshape(2 * pairs, half)

    offsets = list(range(1, (n_ga + 1) // 2))
    moves = {s: [((i - s) % n_ga, i) for i in range(n_ga)] for s in offsets}
    middle = n_ga // 2 if n_ga % 2 == 0 else 0
    owners = []
    if middle:
        owners = [a if a % 2 == 1 else a + middle for a in range(middle)]
        moves[middle] = [((o - middle) % n_ga, o) for o in owners]
        offsets = offsets + [middle]
    received = {s: lax.ppermute(own_cols, "ga", moves[s]) for s in offsets}

    raw = jnp.concatenate([pair_matrix, sibling], 1)
    raw_t = jnp.transpose(raw, (2, 0, 1)).astype(f32)
    re_t, im_t = raw_t[:, 0], raw_t[:, 1]
    forms = []
    for w in range(2):
        forms.append(jnp.concatenate([weight[w] * re_t, weight[w] * im_t], 1))
    for w in range(2):
        forms.append(jnp.concatenate([-(weight[w] * im_t), weight[w] * re_t], 1))
    left = jnp.stack([f.reshape(n_chip, chip_rows, 2 * pairs).astype(bf16) for f in forms], 1)
    left = left.reshape(n_chip, 4 * chip_rows, 2 * pairs)

    def term(right, step):
        target = walk_table[(spot - way * step) % n_chip]
        rows = lax.dynamic_index_in_dim(left, target, 0, keepdims=False)
        return jnp.dot(rows, right, preferred_element_type=f32)

    def ring_sum(right):
        total = term(right, 1)
        for step in range(2, n_chip + 1):
            arrived = lax.ppermute(total.astype(bf16), "pa", ring_route)
            total = term(right, step) + arrived.astype(f32)
        return total.astype(bf16).reshape(4, chip_rows, half)

    def direct(tile):
        low, high = tile[:, :out_rows], tile[:, out_rows:]
        keep = jnp.where(core == 0, low, high)
        got = lax.ppermute(jnp.where(core == 0, high, low), "pa", sibling_route)
        keep = keep.reshape(4, out_rows, n_chip, 1, out_rows)
        got = got.reshape(4, out_rows, n_chip, 1, out_rows)
        first = jnp.where(core == 0, keep, got)
        second = jnp.where(core == 0, got, keep)
        return jnp.concatenate([first, second], 3).reshape(4, out_rows, gblock).astype(f32)

    def mirrored(tile, s):
        pieces = tile.reshape(4, chip_rows, n_chip, out_rows).transpose(2, 0, 1, 3)
        got = []
        for k in range(n_chip):
            route = []
            for source, owner in moves[s]:
                for q in range(n_pa):
                    to = (((q // 2) ^ k) * 2) + q % 2
                    route.append((owner * n_pa + q, source * n_pa + to))
            piece = lax.dynamic_index_in_dim(pieces, chip ^ k, 0, keepdims=False)
            got.append(lax.ppermute(piece, ("ga", "pa"), route))
        got = jnp.stack(got)
        rows = [lax.dynamic_index_in_dim(got, chip ^ c, 0, keepdims=False) for c in range(n_chip)]
        whole = jnp.transpose(jnp.concatenate(rows, 1), (0, 2, 1)).astype(f32)
        return jnp.concatenate([whole[:2], -whole[2:]], 0)

    real = jnp.zeros((2, out_rows, gblock * n_ga), f32)
    imag = jnp.zeros((2, out_rows, gblock * n_ga), f32)

    def put(outs, block, index):
        at = (jnp.int32(0), jnp.int32(0), index * gblock)
        return (lax.dynamic_update_slice(outs[0], block[:2], at), lax.dynamic_update_slice(outs[1], block[2:], at))

    outs = put((real, imag), direct(ring_sum(own_cols)), g)
    for s in offsets:
        tile = ring_sum(received[s])
        if s == middle:
            mine = jnp.zeros((), jnp.bool_)
            for o in owners:
                mine = mine | (g == o)
            block = jnp.where(mine, direct(tile), mirrored(tile, s))
            outs = put(outs, block, (g - s) % n_ga)
        else:
            outs = put(outs, direct(tile), (g - s) % n_ga)
            outs = put(outs, mirrored(tile, s), (g + s) % n_ga)
    return outs


def solution(mesh):
    return jax.shard_map(
        local,
        mesh=mesh,
        in_specs=(P(None, "pa", "ga"), P("pa"), P("pa"), P(), P()),
        out_specs=(P(None, ("ga", "pa"), None), P(None, ("ga", "pa"), None)),
        check_vma=False,
    )
```

```python
import jax
import jax.numpy as jnp
from jax import lax
from jax.experimental import pallas as pl
from jax.experimental.pallas import tpu as pltpu
from jax.sharding import PartitionSpec as P

omega_squared = 4.0


def pair_weights(valence_idx, conduction_idx, e_val, e_cond):
    val_hits = valence_idx[:, None] == jnp.arange(e_val.shape[0], dtype=jnp.int32)[None, :]
    cond_hits = conduction_idx[:, None] == jnp.arange(e_cond.shape[0], dtype=jnp.int32)[None, :]
    picked_val = jnp.sum(jnp.where(val_hits, e_val[None, :], 0.0), 1)
    picked_cond = jnp.sum(jnp.where(cond_hits, e_cond[None, :], 0.0), 1)
    gap = picked_cond - picked_val
    return jnp.stack([-4.0 / gap, -4.0 * gap / (gap * gap + omega_squared)])


def term_kernel(has_arrived, target_ref, left_ref, weight_ref, right_ref, *rest):
    out_ref = rest[-1]
    pairs = weight_ref.shape[2]
    w = weight_ref[0]
    re = (left_ref[0, :, :pairs].astype(jnp.float32) * w).astype(jnp.bfloat16)
    im = (left_ref[0, :, pairs:].astype(jnp.float32) * w).astype(jnp.bfloat16)
    other_re, other_im = right_ref[:pairs], right_ref[pairs:]

    def times(a, b):
        return jnp.dot(a, b, preferred_element_type=jnp.float32)

    real = times(re, other_re) + times(im, other_im)
    imag = times(re, other_im) - times(im, other_re)
    if has_arrived:
        real = real + rest[0][0, 0].astype(jnp.float32)
        imag = imag + rest[0][1, 0].astype(jnp.float32)
    out_ref[0, 0] = real.astype(jnp.bfloat16)
    out_ref[1, 0] = imag.astype(jnp.bfloat16)


def chip_term(target, left, weight, right, arrived):
    n_chip, rows, depth = left.shape
    cols = right.shape[1]
    tile = pl.BlockSpec((2, 1, rows, cols), lambda w, t: (0, w, 0, 0))
    in_specs = [
        pl.BlockSpec((1, rows, depth), lambda w, t: (t[0], 0, 0)),
        pl.BlockSpec((1, 1, depth // 2), lambda w, t: (w, 0, 0)),
        pl.BlockSpec((depth, cols), lambda w, t: (0, 0)),
    ]
    args = [left, weight, right]
    if arrived is not None:
        in_specs.append(tile)
        args.append(arrived)
    return pl.pallas_call(
        lambda *refs: term_kernel(arrived is not None, *refs),
        out_shape=jax.ShapeDtypeStruct((2, 2, rows, cols), jnp.bfloat16),
        grid_spec=pltpu.PrefetchScalarGridSpec(
            num_scalar_prefetch=1, grid=(2,), in_specs=in_specs, out_specs=tile
        ),
        compiler_params=pltpu.CompilerParams(vmem_limit_bytes=40 * 1024 * 1024),
        cost_estimate=pl.CostEstimate(
            flops=8 * rows * cols * depth, bytes_accessed=2 * depth * (rows + cols), transcendentals=0
        ),
        name="chip_term",
    )(target.reshape(1), *args)


def local(pair_matrix, valence_idx, conduction_idx, e_val, e_cond):
    n_ga, n_pa = lax.axis_size("ga"), lax.axis_size("pa")
    g, p = lax.axis_index("ga"), lax.axis_index("pa")
    n_chip = n_pa // 2
    chip, core = p // 2, p % 2
    gblock = pair_matrix.shape[2]
    out_rows = gblock // n_pa
    chip_rows = 2 * out_rows
    half = gblock // 2
    bf16, f32 = jnp.bfloat16, jnp.float32

    walk = list(range(n_chip // 2)) + list(range(n_chip - 1, n_chip // 2 - 1, -1))
    place_of = [walk.index(c) for c in range(n_chip)]
    walk_table = jnp.array(walk, jnp.int32)
    spot = jnp.array(place_of, jnp.int32)[chip]
    way = 1 - 2 * core
    ring_route = []
    for i in range(n_chip):
        ring_route.append((2 * walk[i], 2 * walk[(i + 1) % n_chip]))
        ring_route.append((2 * walk[i] + 1, 2 * walk[(i - 1) % n_chip] + 1))
    sibling_route = [(i, i ^ 1) for i in range(n_pa)]

    def core_columns(x):
        parts = x.reshape(x.shape[:-1] + (n_chip, 2, out_rows))
        picked = jnp.where(core == 0, parts[..., 0, :], parts[..., 1, :])
        return picked.reshape(x.shape[:-1] + (half,))

    sibling = lax.ppermute(pair_matrix, "pa", sibling_route)
    weight = pair_weights(valence_idx, conduction_idx, e_val, e_cond)
    weight = jnp.concatenate([weight, lax.ppermute(weight, "pa", sibling_route)], 1)

    own_cols = jnp.concatenate([core_columns(pair_matrix), core_columns(sibling)], 1)
    pairs = own_cols.shape[1]
    own_cols = own_cols.reshape(2 * pairs, half)

    offsets = list(range(1, (n_ga + 1) // 2))
    moves = {s: [((i - s) % n_ga, i) for i in range(n_ga)] for s in offsets}
    middle = n_ga // 2 if n_ga % 2 == 0 else 0
    owners = []
    if middle:
        owners = [a if a % 2 == 1 else a + middle for a in range(middle)]
        moves[middle] = [((o - middle) % n_ga, o) for o in owners]
        offsets = offsets + [middle]
    received = {s: lax.ppermute(own_cols, "ga", moves[s]) for s in offsets}

    rows_t = jnp.concatenate([jnp.transpose(x[part]) for part in range(2) for x in (pair_matrix, sibling)], 1)
    left = rows_t.reshape(n_chip, chip_rows, 2 * pairs)
    weight = weight.reshape(2, 1, pairs)

    def term(right, step, arrived):
        target = walk_table[(spot - way * step) % n_chip]
        return chip_term(target, left, weight, right, arrived)

    def ring_sum(right):
        total = term(right, 1, None)
        for step in range(2, n_chip + 1):
            total = term(right, step, lax.ppermute(total, "pa", ring_route))
        return total.reshape(4, chip_rows, half)

    def direct(tile):
        low, high = tile[:, :out_rows], tile[:, out_rows:]
        keep = jnp.where(core == 0, low, high)
        got = lax.ppermute(jnp.where(core == 0, high, low), "pa", sibling_route)
        keep = keep.reshape(4, out_rows, n_chip, 1, out_rows)
        got = got.reshape(4, out_rows, n_chip, 1, out_rows)
        first = jnp.where(core == 0, keep, got)
        second = jnp.where(core == 0, got, keep)
        return jnp.concatenate([first, second], 3).reshape(4, out_rows, gblock).astype(f32)

    def mirrored(tile, s):
        pieces = tile.reshape(4, chip_rows, n_chip, out_rows).transpose(2, 0, 1, 3)
        got = []
        for k in range(n_chip):
            route = []
            for source, owner in moves[s]:
                for q in range(n_pa):
                    to = (((q // 2) ^ k) * 2) + q % 2
                    route.append((owner * n_pa + q, source * n_pa + to))
            piece = lax.dynamic_index_in_dim(pieces, chip ^ k, 0, keepdims=False)
            got.append(lax.ppermute(piece, ("ga", "pa"), route))
        got = jnp.stack(got)
        rows = [lax.dynamic_index_in_dim(got, chip ^ c, 0, keepdims=False) for c in range(n_chip)]
        whole = jnp.transpose(jnp.concatenate(rows, 1), (0, 2, 1)).astype(f32)
        return jnp.concatenate([whole[:2], -whole[2:]], 0)

    real = jnp.zeros((2, out_rows, gblock * n_ga), f32)
    imag = jnp.zeros((2, out_rows, gblock * n_ga), f32)

    def put(outs, block, index):
        at = (jnp.int32(0), jnp.int32(0), index * gblock)
        return (lax.dynamic_update_slice(outs[0], block[:2], at), lax.dynamic_update_slice(outs[1], block[2:], at))

    outs = put((real, imag), direct(ring_sum(own_cols)), g)
    for s in offsets:
        tile = ring_sum(received[s])
        if s == middle:
            mine = jnp.zeros((), jnp.bool_)
            for o in owners:
                mine = mine | (g == o)
            block = jnp.where(mine, direct(tile), mirrored(tile, s))
            outs = put(outs, block, (g - s) % n_ga)
        else:
            outs = put(outs, direct(tile), (g - s) % n_ga)
            outs = put(outs, mirrored(tile, s), (g + s) % n_ga)
    return outs


def solution(mesh):
    return jax.shard_map(
        local,
        mesh=mesh,
        in_specs=(P(None, "pa", "ga"), P("pa"), P("pa"), P(), P()),
        out_specs=(P(None, ("ga", "pa"), None), P(None, ("ga", "pa"), None)),
        check_vma=False,
    )
```

```python
import jax
import jax.numpy as jnp
from jax import lax
from jax.experimental import pallas as pl
from jax.experimental.pallas import tpu as pltpu
from jax.sharding import PartitionSpec as P

omega_squared = 4.0


def pair_weights(valence_idx, conduction_idx, e_val, e_cond):
    val_hits = valence_idx[:, None] == jnp.arange(e_val.shape[0], dtype=jnp.int32)[None, :]
    cond_hits = conduction_idx[:, None] == jnp.arange(e_cond.shape[0], dtype=jnp.int32)[None, :]
    picked_val = jnp.sum(jnp.where(val_hits, e_val[None, :], 0.0), 1)
    picked_cond = jnp.sum(jnp.where(cond_hits, e_cond[None, :], 0.0), 1)
    gap = picked_cond - picked_val
    return jnp.stack([-4.0 / gap, -4.0 * gap / (gap * gap + omega_squared)])


def term_kernel(has_arrived, target_ref, left_ref, weight_ref, right_ref, *rest):
    out_ref = rest[-1]
    pairs = weight_ref.shape[2]
    w = weight_ref[0]
    re = (left_ref[0, :, :pairs].astype(jnp.float32) * w).astype(jnp.bfloat16)
    im = (left_ref[0, :, pairs:].astype(jnp.float32) * w).astype(jnp.bfloat16)
    other_re, other_im = right_ref[:pairs], right_ref[pairs:]

    def times(a, b):
        return jnp.dot(a, b, preferred_element_type=jnp.float32)

    real = times(re, other_re) + times(im, other_im)
    imag = times(re, other_im) - times(im, other_re)
    if has_arrived:
        real = real + rest[0][0, 0].astype(jnp.float32)
        imag = imag + rest[0][1, 0].astype(jnp.float32)
    out_ref[0, 0] = real.astype(jnp.bfloat16)
    out_ref[1, 0] = imag.astype(jnp.bfloat16)


def chip_term(target, left, weight, right, arrived):
    n_chip, rows, depth = left.shape
    cols = right.shape[1]
    tile = pl.BlockSpec((2, 1, rows, cols), lambda w, t: (0, w, 0, 0))
    in_specs = [
        pl.BlockSpec((1, rows, depth), lambda w, t: (t[0], 0, 0)),
        pl.BlockSpec((1, 1, depth // 2), lambda w, t: (w, 0, 0)),
        pl.BlockSpec((depth, cols), lambda w, t: (0, 0)),
    ]
    args = [left, weight, right]
    if arrived is not None:
        in_specs.append(tile)
        args.append(arrived)
    return pl.pallas_call(
        lambda *refs: term_kernel(arrived is not None, *refs),
        out_shape=jax.ShapeDtypeStruct((2, 2, rows, cols), jnp.bfloat16),
        grid_spec=pltpu.PrefetchScalarGridSpec(
            num_scalar_prefetch=1, grid=(2,), in_specs=in_specs, out_specs=tile
        ),
        compiler_params=pltpu.CompilerParams(vmem_limit_bytes=40 * 1024 * 1024),
        cost_estimate=pl.CostEstimate(
            flops=8 * rows * cols * depth, bytes_accessed=2 * depth * (rows + cols), transcendentals=0
        ),
        name="chip_term",
    )(target.reshape(1), *args)


def local(pair_matrix, valence_idx, conduction_idx, e_val, e_cond):
    n_ga, n_pa = lax.axis_size("ga"), lax.axis_size("pa")
    g, p = lax.axis_index("ga"), lax.axis_index("pa")
    n_chip = n_pa // 2
    chip, core = p // 2, p % 2
    gblock = pair_matrix.shape[2]
    out_rows = gblock // n_pa
    chip_rows = 2 * out_rows
    half = gblock // 2
    bf16, f32 = jnp.bfloat16, jnp.float32

    walk = list(range(n_chip // 2)) + list(range(n_chip - 1, n_chip // 2 - 1, -1))
    place_of = [walk.index(c) for c in range(n_chip)]
    walk_table = jnp.array(walk, jnp.int32)
    spot = jnp.array(place_of, jnp.int32)[chip]
    way = 1 - 2 * core
    ring_route = []
    for i in range(n_chip):
        ring_route.append((2 * walk[i], 2 * walk[(i + 1) % n_chip]))
        ring_route.append((2 * walk[i] + 1, 2 * walk[(i - 1) % n_chip] + 1))
    sibling_route = [(i, i ^ 1) for i in range(n_pa)]

    def core_columns(x):
        parts = x.reshape(x.shape[:-1] + (n_chip, 2, out_rows))
        picked = jnp.where(core == 0, parts[..., 0, :], parts[..., 1, :])
        return picked.reshape(x.shape[:-1] + (half,))

    sibling = lax.ppermute(pair_matrix, "pa", sibling_route)
    weight = pair_weights(valence_idx, conduction_idx, e_val, e_cond)
    weight = jnp.concatenate([weight, lax.ppermute(weight, "pa", sibling_route)], 1)

    own_cols = jnp.concatenate([core_columns(pair_matrix), core_columns(sibling)], 1)
    pairs = own_cols.shape[1]
    own_cols = own_cols.reshape(2 * pairs, half)

    offsets = list(range(1, (n_ga + 1) // 2))
    moves = {s: [((i - s) % n_ga, i) for i in range(n_ga)] for s in offsets}
    middle = n_ga // 2 if n_ga % 2 == 0 else 0
    owners = []
    if middle:
        owners = [a if a % 2 == 1 else a + middle for a in range(middle)]
        moves[middle] = [((o - middle) % n_ga, o) for o in owners]
        offsets = offsets + [middle]
    rows_t = jnp.concatenate([jnp.transpose(x[part]) for part in range(2) for x in (pair_matrix, sibling)], 1)
    left = rows_t.reshape(n_chip, chip_rows, 2 * pairs)
    weight = weight.reshape(2, 1, pairs)

    def term(right, step, arrived):
        target = walk_table[(spot - way * step) % n_chip]
        return chip_term(target, left, weight, right, arrived)

    def ring_sum(right):
        total = term(right, 1, None)
        for step in range(2, n_chip + 1):
            total = term(right, step, lax.ppermute(total, "pa", ring_route))
        return total.reshape(4, chip_rows, half)

    own_tile = ring_sum(own_cols)
    received, sent = {}, own_cols
    for s in offsets:
        if received:
            sent, received[s - 1], own_tile = lax.optimization_barrier((sent, received[s - 1], own_tile))
        received[s] = lax.ppermute(sent, "ga", moves[s])

    def direct(tile):
        low, high = tile[:, :out_rows], tile[:, out_rows:]
        keep = jnp.where(core == 0, low, high)
        got = lax.ppermute(jnp.where(core == 0, high, low), "pa", sibling_route)
        keep = keep.reshape(4, out_rows, n_chip, 1, out_rows)
        got = got.reshape(4, out_rows, n_chip, 1, out_rows)
        first = jnp.where(core == 0, keep, got)
        second = jnp.where(core == 0, got, keep)
        return jnp.concatenate([first, second], 3).reshape(4, out_rows, gblock)

    def mirrored(tile, s):
        pieces = tile.reshape(4, chip_rows, n_chip, out_rows).transpose(2, 0, 1, 3)
        got = []
        for k in range(n_chip):
            route = []
            for source, owner in moves[s]:
                for q in range(n_pa):
                    to = (((q // 2) ^ k) * 2) + q % 2
                    route.append((owner * n_pa + q, source * n_pa + to))
            piece = lax.dynamic_index_in_dim(pieces, chip ^ k, 0, keepdims=False)
            got.append(lax.ppermute(piece, ("ga", "pa"), route))
        got = jnp.stack(got)
        rows = [lax.dynamic_index_in_dim(got, chip ^ c, 0, keepdims=False) for c in range(n_chip)]
        whole = jnp.transpose(jnp.concatenate(rows, 1), (0, 2, 1))
        return jnp.concatenate([whole[:2], -whole[2:]], 0)

    real = jnp.zeros((2, out_rows, gblock * n_ga), f32)
    imag = jnp.zeros((2, out_rows, gblock * n_ga), f32)

    def put(outs, block, index):
        block = block.astype(f32)
        at = (jnp.int32(0), jnp.int32(0), index * gblock)
        return (lax.dynamic_update_slice(outs[0], block[:2], at), lax.dynamic_update_slice(outs[1], block[2:], at))

    outs = put((real, imag), direct(own_tile), g)
    previous = own_tile
    for s in offsets:
        right, previous = lax.optimization_barrier((received[s], previous))
        tile = previous = ring_sum(right)
        if s == middle:
            mine = jnp.zeros((), jnp.bool_)
            for o in owners:
                mine = mine | (g == o)
            block = jnp.where(mine, direct(tile), mirrored(tile, s))
            outs = put(outs, block, (g - s) % n_ga)
        else:
            outs = put(outs, direct(tile), (g - s) % n_ga)
            outs = put(outs, mirrored(tile, s), (g + s) % n_ga)
    return outs


def solution(mesh):
    return jax.shard_map(
        local,
        mesh=mesh,
        in_specs=(P(None, "pa", "ga"), P("pa"), P("pa"), P(), P()),
        out_specs=(P(None, ("ga", "pa"), None), P(None, ("ga", "pa"), None)),
        check_vma=False,
    )
```

```python
import jax
import jax.numpy as jnp
from jax import lax
from jax.experimental import pallas as pl
from jax.experimental.pallas import tpu as pltpu
from jax.sharding import PartitionSpec as P

omega_squared = 4.0


def pair_weights(valence_idx, conduction_idx, e_val, e_cond):
    val_hits = valence_idx[:, None] == jnp.arange(e_val.shape[0], dtype=jnp.int32)[None, :]
    cond_hits = conduction_idx[:, None] == jnp.arange(e_cond.shape[0], dtype=jnp.int32)[None, :]
    picked_val = jnp.sum(jnp.where(val_hits, e_val[None, :], 0.0), 1)
    picked_cond = jnp.sum(jnp.where(cond_hits, e_cond[None, :], 0.0), 1)
    gap = picked_cond - picked_val
    return jnp.stack([-4.0 / gap, -4.0 * gap / (gap * gap + omega_squared)])


def term_kernel(has_arrived, target_ref, left_ref, weight_ref, right_ref, *rest):
    out_ref = rest[-1]
    pairs = weight_ref.shape[2]
    w = weight_ref[0]
    re = (left_ref[0, :, :pairs].astype(jnp.float32) * w).astype(jnp.bfloat16)
    im = (left_ref[0, :, pairs:].astype(jnp.float32) * w).astype(jnp.bfloat16)
    other_re, other_im = right_ref[:pairs], right_ref[pairs:]

    def times(a, b):
        return jnp.dot(a, b, preferred_element_type=jnp.float32)

    real = times(re, other_re) + times(im, other_im)
    imag = times(re, other_im) - times(im, other_re)
    if has_arrived:
        real = real + rest[0][0, 0].astype(jnp.float32)
        imag = imag + rest[0][1, 0].astype(jnp.float32)
    out_ref[0, 0] = real.astype(jnp.bfloat16)
    out_ref[1, 0] = imag.astype(jnp.bfloat16)


def chip_term(target, left, weight, right, arrived):
    n_chip, rows, depth = left.shape
    cols = right.shape[1]
    tile = pl.BlockSpec((2, 1, rows, cols), lambda w, t: (0, w, 0, 0))
    in_specs = [
        pl.BlockSpec((1, rows, depth), lambda w, t: (t[0], 0, 0)),
        pl.BlockSpec((1, 1, depth // 2), lambda w, t: (w, 0, 0)),
        pl.BlockSpec((depth, cols), lambda w, t: (0, 0)),
    ]
    args = [left, weight, right]
    if arrived is not None:
        in_specs.append(tile)
        args.append(arrived)
    return pl.pallas_call(
        lambda *refs: term_kernel(arrived is not None, *refs),
        out_shape=jax.ShapeDtypeStruct((2, 2, rows, cols), jnp.bfloat16),
        grid_spec=pltpu.PrefetchScalarGridSpec(
            num_scalar_prefetch=1, grid=(2,), in_specs=in_specs, out_specs=tile
        ),
        compiler_params=pltpu.CompilerParams(vmem_limit_bytes=40 * 1024 * 1024),
        cost_estimate=pl.CostEstimate(
            flops=8 * rows * cols * depth, bytes_accessed=2 * depth * (rows + cols), transcendentals=0
        ),
        name="chip_term",
    )(target.reshape(1), *args)


def local(pair_matrix, valence_idx, conduction_idx, e_val, e_cond):
    n_ga, n_pa = lax.axis_size("ga"), lax.axis_size("pa")
    g, p = lax.axis_index("ga"), lax.axis_index("pa")
    n_chip = n_pa // 2
    chip, core = p // 2, p % 2
    gblock = pair_matrix.shape[2]
    out_rows = gblock // n_pa
    chip_rows = 2 * out_rows
    half = gblock // 2
    bf16, f32 = jnp.bfloat16, jnp.float32

    walk = list(range(n_chip // 2)) + list(range(n_chip - 1, n_chip // 2 - 1, -1))
    place_of = [walk.index(c) for c in range(n_chip)]
    walk_table = jnp.array(walk, jnp.int32)
    spot = jnp.array(place_of, jnp.int32)[chip]
    way = 1 - 2 * core
    ring_route = []
    for i in range(n_chip):
        ring_route.append((2 * walk[i], 2 * walk[(i + 1) % n_chip]))
        ring_route.append((2 * walk[i] + 1, 2 * walk[(i - 1) % n_chip] + 1))
    sibling_route = [(i, i ^ 1) for i in range(n_pa)]

    def core_columns(x):
        parts = x.reshape(x.shape[:-1] + (n_chip, 2, out_rows))
        picked = jnp.where(core == 0, parts[..., 0, :], parts[..., 1, :])
        return picked.reshape(x.shape[:-1] + (half,))

    sibling = lax.ppermute(pair_matrix, "pa", sibling_route)
    weight = pair_weights(valence_idx, conduction_idx, e_val, e_cond)
    weight = jnp.concatenate([weight, lax.ppermute(weight, "pa", sibling_route)], 1)

    own_cols = jnp.concatenate([core_columns(pair_matrix), core_columns(sibling)], 1)
    pairs = own_cols.shape[1]
    own_cols = own_cols.reshape(2 * pairs, half)

    offsets = list(range(1, (n_ga + 1) // 2))
    moves = {s: [((i - s) % n_ga, i) for i in range(n_ga)] for s in offsets}
    middle = n_ga // 2 if n_ga % 2 == 0 else 0
    owners = []
    if middle:
        owners = [a if a % 2 == 1 else a + middle for a in range(middle)]
        moves[middle] = [((o - middle) % n_ga, o) for o in owners]
        offsets = offsets + [middle]
    rows_t = jnp.concatenate([jnp.transpose(x[part]) for part in range(2) for x in (pair_matrix, sibling)], 1)
    left = rows_t.reshape(n_chip, chip_rows, 2 * pairs)
    weight = weight.reshape(2, 1, pairs)

    def term(right, step, arrived):
        target = walk_table[(spot - way * step) % n_chip]
        return chip_term(target, left, weight, right, arrived)

    def ring_sum(right):
        total = term(right, 1, None)
        for step in range(2, n_chip + 1):
            total = term(right, step, lax.ppermute(total, "pa", ring_route))
        return total.reshape(4, chip_rows, half)

    own_tile = ring_sum(own_cols)
    received, sent = {}, own_cols
    for s in offsets:
        if received:
            sent, received[s - 1], own_tile = lax.optimization_barrier((sent, received[s - 1], own_tile))
        received[s] = lax.ppermute(sent, "ga", moves[s])

    def direct(tile):
        low, high = tile[:, :out_rows], tile[:, out_rows:]
        keep = jnp.where(core == 0, low, high)
        got = lax.ppermute(jnp.where(core == 0, high, low), "pa", sibling_route)
        keep = keep.reshape(4, out_rows, n_chip, 1, out_rows)
        got = got.reshape(4, out_rows, n_chip, 1, out_rows)
        first = jnp.where(core == 0, keep, got)
        second = jnp.where(core == 0, got, keep)
        return jnp.concatenate([first, second], 3).reshape(4, out_rows, gblock)

    def mirrored(tile, s):
        pieces = tile.reshape(4, chip_rows, n_chip, out_rows).transpose(2, 0, 1, 3)
        got = []
        for k in range(n_chip):
            route = []
            for source, owner in moves[s]:
                for q in range(n_pa):
                    to = (((q // 2) ^ k) * 2) + q % 2
                    route.append((owner * n_pa + q, source * n_pa + to))
            piece = lax.dynamic_index_in_dim(pieces, chip ^ k, 0, keepdims=False)
            got.append(lax.ppermute(piece, ("ga", "pa"), route))
        got = jnp.stack(got)
        rows = [lax.dynamic_index_in_dim(got, chip ^ c, 0, keepdims=False) for c in range(n_chip)]
        whole = jnp.transpose(jnp.concatenate(rows, 1), (0, 2, 1))
        return jnp.concatenate([whole[:2], -whole[2:]], 0)

    real = jnp.zeros((2, out_rows, gblock * n_ga), f32)
    imag = jnp.zeros((2, out_rows, gblock * n_ga), f32)

    def put(outs, block, index):
        block = block.astype(f32)
        at = (jnp.int32(0), jnp.int32(0), index * gblock)
        return (lax.dynamic_update_slice(outs[0], block[:2], at), lax.dynamic_update_slice(outs[1], block[2:], at))

    outs = put((real, imag), direct(own_tile), g)
    previous = own_tile
    for s in offsets:
        right, previous = lax.optimization_barrier((received[s], previous))
        if s > 1:
            right, outs = lax.optimization_barrier((right, outs))
        tile = previous = ring_sum(right)
        if s == middle:
            mine = jnp.zeros((), jnp.bool_)
            for o in owners:
                mine = mine | (g == o)
            block = jnp.where(mine, direct(tile), mirrored(tile, s))
            outs = put(outs, block, (g - s) % n_ga)
        else:
            outs = put(outs, direct(tile), (g - s) % n_ga)
            outs = put(outs, mirrored(tile, s), (g + s) % n_ga)
    return outs


def solution(mesh):
    return jax.shard_map(
        local,
        mesh=mesh,
        in_specs=(P(None, "pa", "ga"), P("pa"), P("pa"), P(), P()),
        out_specs=(P(None, ("ga", "pa"), None), P(None, ("ga", "pa"), None)),
        check_vma=False,
    )
```

```python
import jax
import jax.numpy as jnp
from jax import lax
from jax.experimental import pallas as pl
from jax.experimental.pallas import tpu as pltpu
from jax.sharding import PartitionSpec as P

omega_squared = 4.0


def pair_weights(valence_idx, conduction_idx, e_val, e_cond):
    val_hits = valence_idx[:, None] == jnp.arange(e_val.shape[0], dtype=jnp.int32)[None, :]
    cond_hits = conduction_idx[:, None] == jnp.arange(e_cond.shape[0], dtype=jnp.int32)[None, :]
    picked_val = jnp.sum(jnp.where(val_hits, e_val[None, :], 0.0), 1)
    picked_cond = jnp.sum(jnp.where(cond_hits, e_cond[None, :], 0.0), 1)
    gap = picked_cond - picked_val
    return jnp.stack([-4.0 / gap, -4.0 * gap / (gap * gap + omega_squared)])


def term_kernel(has_arrived, target_ref, left_ref, weight_ref, right_ref, *rest):
    out_ref = rest[-1]
    pairs = weight_ref.shape[2]
    w = weight_ref[0]
    re = (left_ref[0, :, :pairs].astype(jnp.float32) * w).astype(jnp.bfloat16)
    im = (left_ref[0, :, pairs:].astype(jnp.float32) * w).astype(jnp.bfloat16)
    other_re, other_im = right_ref[:pairs], right_ref[pairs:]

    def times(a, b):
        return jnp.dot(a, b, preferred_element_type=jnp.float32)

    real = times(re, other_re) + times(im, other_im)
    imag = times(re, other_im) - times(im, other_re)
    if has_arrived:
        real = real + rest[0][0, 0].astype(jnp.float32)
        imag = imag + rest[0][1, 0].astype(jnp.float32)
    out_ref[0, 0] = real.astype(jnp.bfloat16)
    out_ref[1, 0] = imag.astype(jnp.bfloat16)


def chip_term(target, left, weight, right, arrived):
    n_chip, rows, depth = left.shape
    cols = right.shape[1]
    tile = pl.BlockSpec((2, 1, rows, cols), lambda w, t: (0, w, 0, 0))
    in_specs = [
        pl.BlockSpec((1, rows, depth), lambda w, t: (t[0], 0, 0)),
        pl.BlockSpec((1, 1, depth // 2), lambda w, t: (w, 0, 0)),
        pl.BlockSpec((depth, cols), lambda w, t: (0, 0)),
    ]
    args = [left, weight, right]
    if arrived is not None:
        in_specs.append(tile)
        args.append(arrived)
    return pl.pallas_call(
        lambda *refs: term_kernel(arrived is not None, *refs),
        out_shape=jax.ShapeDtypeStruct((2, 2, rows, cols), jnp.bfloat16),
        grid_spec=pltpu.PrefetchScalarGridSpec(
            num_scalar_prefetch=1, grid=(2,), in_specs=in_specs, out_specs=tile
        ),
        compiler_params=pltpu.CompilerParams(vmem_limit_bytes=40 * 1024 * 1024),
        cost_estimate=pl.CostEstimate(
            flops=8 * rows * cols * depth, bytes_accessed=2 * depth * (rows + cols), transcendentals=0
        ),
        name="chip_term",
    )(target.reshape(1), *args)


def local(pair_matrix, valence_idx, conduction_idx, e_val, e_cond):
    n_ga, n_pa = lax.axis_size("ga"), lax.axis_size("pa")
    g, p = lax.axis_index("ga"), lax.axis_index("pa")
    n_chip = n_pa // 2
    chip, core = p // 2, p % 2
    gblock = pair_matrix.shape[2]
    out_rows = gblock // n_pa
    chip_rows = 2 * out_rows
    half = gblock // 2
    bf16, f32 = jnp.bfloat16, jnp.float32

    walk = list(range(n_chip // 2)) + list(range(n_chip - 1, n_chip // 2 - 1, -1))
    place_of = [walk.index(c) for c in range(n_chip)]
    walk_table = jnp.array(walk, jnp.int32)
    spot = jnp.array(place_of, jnp.int32)[chip]
    way = 1 - 2 * core
    ring_route = []
    for i in range(n_chip):
        ring_route.append((2 * walk[i], 2 * walk[(i + 1) % n_chip]))
        ring_route.append((2 * walk[i] + 1, 2 * walk[(i - 1) % n_chip] + 1))
    sibling_route = [(i, i ^ 1) for i in range(n_pa)]

    def core_columns(x):
        parts = x.reshape(x.shape[:-1] + (n_chip, 2, out_rows))
        picked = jnp.where(core == 0, parts[..., 0, :], parts[..., 1, :])
        return picked.reshape(x.shape[:-1] + (half,))

    sibling = lax.ppermute(pair_matrix, "pa", sibling_route)
    weight = pair_weights(valence_idx, conduction_idx, e_val, e_cond)
    weight = jnp.concatenate([weight, lax.ppermute(weight, "pa", sibling_route)], 1)

    own_cols = jnp.concatenate([core_columns(pair_matrix), core_columns(sibling)], 1)
    pairs = own_cols.shape[1]
    own_cols = own_cols.reshape(2 * pairs, half)

    offsets = list(range(1, (n_ga + 1) // 2))
    moves = {s: [((i - s) % n_ga, i) for i in range(n_ga)] for s in offsets}
    middle = n_ga // 2 if n_ga % 2 == 0 else 0
    owners = []
    if middle:
        owners = [a if a % 2 == 1 else a + middle for a in range(middle)]
        moves[middle] = [((o - middle) % n_ga, o) for o in owners]
        offsets = offsets + [middle]
    rows_t = jnp.concatenate([jnp.transpose(x[part]) for part in range(2) for x in (pair_matrix, sibling)], 1)
    left = rows_t.reshape(n_chip, chip_rows, 2 * pairs)
    weight = weight.reshape(2, 1, pairs)

    def term(right, step, arrived):
        target = walk_table[(spot - way * step) % n_chip]
        return chip_term(target, left, weight, right, arrived)

    def ring_sum(right):
        total = term(right, 1, None)
        for step in range(2, n_chip + 1):
            total = term(right, step, lax.ppermute(total, "pa", ring_route))
        return total.reshape(4, chip_rows, half)

    own_tile = ring_sum(own_cols)
    received, sent = {}, own_cols
    for s in offsets:
        if received:
            sent, received[s - 1], own_tile = lax.optimization_barrier((sent, received[s - 1], own_tile))
        received[s] = lax.ppermute(sent, "ga", moves[s])

    def direct(tile):
        low, high = tile[:, :out_rows], tile[:, out_rows:]
        keep = jnp.where(core == 0, low, high)
        got = lax.ppermute(jnp.where(core == 0, high, low), "pa", sibling_route)
        keep = keep.reshape(4, out_rows, n_chip, 1, out_rows)
        got = got.reshape(4, out_rows, n_chip, 1, out_rows)
        first = jnp.where(core == 0, keep, got)
        second = jnp.where(core == 0, got, keep)
        return jnp.concatenate([first, second], 3).reshape(4, out_rows, gblock)

    def mirrored(tile, s):
        pieces = tile.reshape(4, chip_rows, n_chip, out_rows).transpose(2, 0, 1, 3)
        got = []
        for k in range(n_chip):
            route = []
            for source, owner in moves[s]:
                for q in range(n_pa):
                    to = (((q // 2) ^ k) * 2) + q % 2
                    route.append((owner * n_pa + q, source * n_pa + to))
            piece = lax.dynamic_index_in_dim(pieces, chip ^ k, 0, keepdims=False)
            got.append(lax.ppermute(piece, ("ga", "pa"), route))
        got = jnp.stack(got)
        rows = [lax.dynamic_index_in_dim(got, chip ^ c, 0, keepdims=False) for c in range(n_chip)]
        whole = jnp.transpose(jnp.concatenate(rows, 1), (0, 2, 1))
        return jnp.concatenate([whole[:2], -whole[2:]], 0)

    real = jnp.zeros((2, out_rows, gblock * n_ga), f32)
    imag = jnp.zeros((2, out_rows, gblock * n_ga), f32)

    def put(outs, block, index):
        block = block.astype(f32)
        at = (jnp.int32(0), jnp.int32(0), index * gblock)
        return (lax.dynamic_update_slice(outs[0], block[:2], at), lax.dynamic_update_slice(outs[1], block[2:], at))

    outs = (real, imag)
    own_block = direct(own_tile)
    previous = own_tile
    for s in offsets:
        right, previous = lax.optimization_barrier((received[s], previous))
        if s > 1:
            right, own_block = lax.optimization_barrier((right, own_block))
        tile = previous = ring_sum(right)
        if s == middle:
            mine = jnp.zeros((), jnp.bool_)
            for o in owners:
                mine = mine | (g == o)
            block = jnp.where(mine, direct(tile), mirrored(tile, s))
            outs = put(outs, block, (g - s) % n_ga)
        else:
            outs = put(outs, direct(tile), (g - s) % n_ga)
            outs = put(outs, mirrored(tile, s), (g + s) % n_ga)
    return put(outs, own_block, g)


def solution(mesh):
    return jax.shard_map(
        local,
        mesh=mesh,
        in_specs=(P(None, "pa", "ga"), P("pa"), P("pa"), P(), P()),
        out_specs=(P(None, ("ga", "pa"), None), P(None, ("ga", "pa"), None)),
        check_vma=False,
    )
```
